32 devices in a mesh: groups: 2 (over y), wide: 8 (over z, x), narrow: 2 (over core).
Axes of the slice: x: 2, y: 2, z: 4, core: 2. Of those that a mesh axis runs over, the one named last changes fastest.
Arguments:
- inputs: bfloat16 [8192, 1024], P(('groups', 'wide', 'narrow')), parts along dimension 0, may hold values from -6 to 6
- filter_taps: bfloat16 [4096, 1024], P(('wide', 'narrow')), may hold values from -6 to 6
- grad_out: bfloat16 [8192, 1024], P(('groups', 'wide', 'narrow')), parts along dimension 0, may hold values from -6 to 6
Outputs:
- outputs: bfloat16 [8192, 1024], P(('groups', 'wide', 'narrow')), parts along dimension 0
- grad_inputs: bfloat16 [8192, 1024], P(('groups', 'wide', 'narrow')), parts along dimension 0
- grad_taps: bfloat16 [8192, 1024], P(('groups', 'wide', 'narrow')), parts along dimension 0
The draws below stay inside these ranges and needn't reach their ends.
There are 2 independent parts, one for each index of `groups`. The reference program is written for one: setup_inputs(seed, part) draws one part's arguments, and reference() takes and returns one part's arrays. A program takes and returns all parts, laid end to end along the dimension named above; an argument that names none is the same for every part. Nothing has to cross between parts.
All inputs are finite; a program needn't handle non-finite values.
Results may differ from the reference program's by a relative error of at most 0.008.
Values may be sent and summed in bfloat16 or wider, within the bound.
A program may use at most 64 MiB of HBM per device.

```python
import math
import jax
import jax.numpy as jnp
from jax import lax

D = 1024
BLOCK = 256
SPAN = 8
SEQ = 4096


def block_scale(stream_key, shape, split, smallest, largest):
    level, own = 1.0, jax.random.fold_in(stream_key, 6)
    for dim, shards_of in split:
        heights = jnp.exp(jax.random.uniform(jax.random.fold_in(own, dim), (shards_of,), jnp.float32, smallest / len(split), largest / len(split)))
        level = level * jnp.repeat(heights, shape[dim] // shards_of).reshape([-1 if axis == dim else 1 for axis in range(len(shape))])
    return level


def scatter_about(stream_key, dims, deviation, most, shards=(), kind=jnp.bfloat16):
    level = block_scale(stream_key, dims, shards, -0.22, 0.18) if shards else 1.0
    result = jax.random.normal(stream_key, dims, jnp.float32) * deviation * level
    return jnp.minimum(jnp.maximum(result, -most), most).astype(kind)


def setup_inputs(seed: int = 0, part: int = 0) -> dict:
    streams_of = jax.random.split(jax.random.key(seed), 4)
    own_keys = jax.random.split(jax.random.fold_in(streams_of[3], part), 4)
    inputs = scatter_about(own_keys[0], (SEQ, D), 1.0, 6.0, ((0, 16),))
    filter_taps = scatter_about(streams_of[1], (SEQ, D), 1.0, 6.0, ((0, 16),))
    grad_out = scatter_about(own_keys[2], (SEQ, D), 1.0, 6.0, ((0, 16),))
    return {"inputs": inputs, "filter_taps": filter_taps, "grad_out": grad_out}


def rounded(values):
    return lax.optimization_barrier(values.astype(jnp.bfloat16)).astype(jnp.float32)

def long_tables(period):
    counter = jnp.arange(period, dtype=jnp.int32)
    product = counter[:, None] * counter[None, :] % period
    angles = product.astype(jnp.float32) * (2.0 * math.pi / period)
    return (rounded(jnp.cos(angles)), rounded(jnp.sin(angles)))

def block_tables(blocksize):
    parity = jnp.arange(2, dtype=jnp.int32)[:, None, None]
    row_index = jnp.arange(blocksize, dtype=jnp.int32)[None, :, None]
    col_index = jnp.arange(blocksize, dtype=jnp.int32)[None, None, :]
    product = row_index * (2 * col_index + parity) % (2 * blocksize)
    angles = product.astype(jnp.float32) * (math.pi / blocksize)
    return (rounded(jnp.cos(angles)), rounded(jnp.sin(angles)))

def twist_tables(span_count, blocksize, seq_len):
    rows = jnp.arange(span_count, dtype=jnp.int32)[:, None, None]
    halves = jnp.arange(2, dtype=jnp.int32)[None, :, None]
    lanes = jnp.arange(blocksize, dtype=jnp.int32)[None, None, :]
    product = (halves * blocksize + lanes) * rows
    angles = product.astype(jnp.float32) * (2.0 * math.pi / seq_len)
    return (jnp.cos(angles), jnp.sin(angles))

def contract(form, table, values):
    return jnp.einsum(form, table, values, precision=lax.Precision.HIGHEST)

def transform(signal, tables):
    long_cos, long_sin, block_cos, block_sin, twist_cos, twist_sin = tables
    shaped = signal.astype(jnp.float32).reshape(SPAN, 2, BLOCK, signal.shape[1])
    first_re = contract('ka,anjc->knjc', long_cos, shaped)
    first_im = -contract('ka,anjc->knjc', long_sin, shaped)
    tw_cos = twist_cos[..., None]
    tw_sin = twist_sin[..., None]
    twisted_re = rounded(first_re * tw_cos + first_im * tw_sin)
    twisted_im = rounded(first_im * tw_cos - first_re * tw_sin)
    paired_re = rounded(jnp.stack([twisted_re[:, 0] + twisted_re[:, 1], twisted_re[:, 0] - twisted_re[:, 1]], axis=1))
    paired_im = rounded(jnp.stack([twisted_im[:, 0] + twisted_im[:, 1], twisted_im[:, 0] - twisted_im[:, 1]], axis=1))
    spec_re = contract('rjq,krjc->krqc', block_cos, paired_re) + contract('rjq,krjc->krqc', block_sin, paired_im)
    spec_im = contract('rjq,krjc->krqc', block_cos, paired_im) - contract('rjq,krjc->krqc', block_sin, paired_re)
    return (spec_re, spec_im)

def invert(spec_re, spec_im, tables):
    long_cos, long_sin, block_cos, block_sin, twist_cos, twist_sin = tables
    unfolded_re = rounded(contract('rjq,krqc->krjc', block_cos, spec_re) - contract('rjq,krqc->krjc', block_sin, spec_im))
    unfolded_im = rounded(contract('rjq,krqc->krjc', block_cos, spec_im) + contract('rjq,krqc->krjc', block_sin, spec_re))
    comb_re = jnp.stack([unfolded_re[:, 0] + unfolded_re[:, 1], unfolded_re[:, 0] - unfolded_re[:, 1]], axis=1)
    comb_im = jnp.stack([unfolded_im[:, 0] + unfolded_im[:, 1], unfolded_im[:, 0] - unfolded_im[:, 1]], axis=1)
    tw_cos = twist_cos[..., None]
    tw_sin = twist_sin[..., None]
    merged_re = rounded(comb_re * tw_cos - comb_im * tw_sin)
    merged_im = rounded(comb_im * tw_cos + comb_re * tw_sin)
    summed = contract('ak,knjc->anjc', long_cos, merged_re) - contract('ak,knjc->anjc', long_sin, merged_im)
    return (summed * (1.0 / SEQ)).astype(jnp.bfloat16).reshape(SEQ, spec_re.shape[3])

def reference(inputs, filter_taps, grad_out):
    long_cos, long_sin = long_tables(SPAN)
    block_cos, block_sin = block_tables(BLOCK)
    twist_cos, twist_sin = twist_tables(SPAN, BLOCK, SEQ)
    tables = (long_cos, long_sin, block_cos, block_sin, twist_cos, twist_sin)
    kernel_scale = 1.0 / math.sqrt(SEQ)
    block_count = D // 128

    def per_block(arrays):
        signal_block, taps_block, cotangent_block = arrays
        input_re, input_im = transform(signal_block, tables)
        kernel_re, kernel_im = transform(taps_block, tables)
        kernel_re = kernel_re * kernel_scale
        kernel_im = kernel_im * kernel_scale
        grad_re, grad_im = transform(cotangent_block, tables)
        fwd_re = rounded(kernel_re * input_re - kernel_im * input_im)
        fwd_im = rounded(kernel_re * input_im + kernel_im * input_re)
        result_out = invert(fwd_re, fwd_im, tables)
        dinp_re = rounded(kernel_re * grad_re + kernel_im * grad_im)
        dinp_im = rounded(kernel_re * grad_im - kernel_im * grad_re)
        result_inputs = invert(dinp_re, dinp_im, tables)
        dtap_re = rounded((input_re * grad_re + input_im * grad_im) * kernel_scale)
        dtap_im = rounded((input_re * grad_im - input_im * grad_re) * kernel_scale)
        result_taps = invert(dtap_re, dtap_im, tables)
        return (result_out, result_inputs, result_taps)

    def split_blocks(array):
        return jnp.transpose(array.reshape(SEQ, block_count, 128), (1, 0, 2))

    def join_blocks(array):
        return jnp.transpose(array, (1, 0, 2)).reshape(SEQ, D)
    results = lax.map(per_block, (split_blocks(inputs), split_blocks(filter_taps), split_blocks(grad_out)))
    return (join_blocks(results[0]), join_blocks(results[1]), join_blocks(results[2]))
```

```python
import math

import jax
import jax.numpy as jnp
import ml_dtypes
import numpy as np
from jax import lax
from jax.experimental import pallas as pl
from jax.experimental.pallas import tpu as pltpu
from jax.sharding import PartitionSpec as P


def partner_2(value, axis, distance):
    mask = 2**distance
    pairs = [(source, source ^ mask) for source in range(lax.axis_size(axis))]
    return lax.ppermute(value, axis, pairs)


def on_device(inputs, filter_taps, grad_out):
    span_count = lax.axis_size("wide")
    blocksize = inputs.shape[0]
    channels = inputs.shape[1]
    shares = channels // span_count
    row_count = span_count * shares
    seq_len = span_count * 2 * blocksize
    parity = lax.axis_index("narrow")
    signed = (1 - 2 * parity).astype(jnp.float32)
    counter = jnp.arange(span_count, dtype=jnp.int32)
    long_angles = (counter[:, None] * counter[None, :] % span_count).astype(jnp.float32) * (
        2.0 * math.pi / span_count
    )
    long_cos = jnp.cos(long_angles)
    long_sin = jnp.sin(long_angles)
    long_forward = jnp.concatenate([long_cos, -long_sin], axis=0).astype(jnp.bfloat16)
    long_inverse = jnp.concatenate([long_cos, -long_sin], axis=1).astype(jnp.bfloat16)
    positions = jnp.arange(blocksize, dtype=jnp.int32)

    def first_section(pieces, twist_cos, twist_sin):
        share_count = pieces.shape[1]
        lane_count = pieces.shape[2]
        flatten = pieces.reshape(span_count, share_count * lane_count)
        mixture = jnp.dot(long_forward, flatten, preferred_element_type=jnp.float32)
        mixture = mixture.reshape(2, span_count, share_count, lane_count)
        real_part = mixture[0] * twist_cos + mixture[1] * twist_sin
        imag_part = mixture[1] * twist_cos - mixture[0] * twist_sin
        return jnp.stack([real_part, imag_part]).astype(jnp.bfloat16)

    def long_back(combined_re, combined_im, twist_cos, twist_sin):
        merged_re = combined_re * twist_cos - combined_im * twist_sin
        merged_im = combined_im * twist_cos + combined_re * twist_sin
        share_count = combined_re.shape[1]
        lane_count = combined_re.shape[2]
        stacked = (
            jnp.stack([merged_re, merged_im])
            .astype(jnp.bfloat16)
            .reshape(2 * span_count, share_count * lane_count)
        )
        summed = jnp.dot(long_inverse, stacked, preferred_element_type=jnp.float32) * (
            1.0 / seq_len
        )
        return summed.astype(jnp.bfloat16).reshape(span_count, share_count, lane_count)

    block_product = positions[:, None] * (2 * positions[None, :] + parity) % (2 * blocksize)
    block_angles = block_product.astype(jnp.float32) * (math.pi / blocksize)
    block_cos = jnp.cos(block_angles)
    block_sin = jnp.sin(block_angles)
    forward_mat = jnp.concatenate(
        [
            jnp.concatenate([block_cos, -block_sin], axis=1),
            jnp.concatenate([block_sin, block_cos], axis=1),
        ],
        axis=0,
    ).astype(jnp.bfloat16)
    cos_turned = jnp.transpose(block_cos)
    sin_turned = jnp.transpose(block_sin)
    inverse_mat = jnp.concatenate(
        [
            jnp.concatenate([cos_turned, sin_turned], axis=1),
            jnp.concatenate([-sin_turned, cos_turned], axis=1),
        ],
        axis=0,
    ).astype(jnp.bfloat16)
    twist_product = (parity * blocksize + positions)[None, None, :] * counter[:, None, None]
    twist_angles = twist_product.astype(jnp.float32) * (2.0 * math.pi / seq_len)
    twist_cos = jnp.cos(twist_angles)
    twist_sin = jnp.sin(twist_angles)

    def section_pairs(pieces):
        return first_section(pieces, twist_cos, twist_sin)

    def spectrum(signal):
        arranged = jnp.transpose(signal).reshape(span_count, shares, blocksize)
        twisted = section_pairs(
            lax.all_to_all(arranged, "wide", split_axis=0, concat_axis=0, tiled=True)
        )
        partner = partner_2(twisted, "narrow", 0)
        paired = (signed * twisted.astype(jnp.float32) + partner.astype(jnp.float32)).astype(
            jnp.bfloat16
        )
        joined = jnp.concatenate(
            [paired[0].reshape(row_count, blocksize), paired[1].reshape(row_count, blocksize)],
            axis=1,
        )
        return jnp.dot(joined, forward_mat, preferred_element_type=jnp.float32)

    def invert(spectrum_in):
        unfolded = jnp.dot(spectrum_in, inverse_mat, preferred_element_type=jnp.float32).astype(
            jnp.bfloat16
        )
        partner = partner_2(unfolded, "narrow", 0)
        combined = signed * unfolded.astype(jnp.float32) + partner.astype(jnp.float32)
        comb_re = combined[:, :blocksize].reshape(span_count, shares, blocksize)
        comb_im = combined[:, blocksize:].reshape(span_count, shares, blocksize)
        arranged = long_back(comb_re, comb_im, twist_cos, twist_sin)
        returned = lax.all_to_all(arranged, "wide", split_axis=0, concat_axis=1, tiled=True)
        return jnp.transpose(returned.reshape(channels, blocksize))

    def product(left_side, right_side, conjugate, factor):
        left_re = left_side[..., :blocksize]
        left_im = left_side[..., blocksize:]
        right_re = right_side[..., :blocksize]
        right_im = right_side[..., blocksize:]
        if conjugate:
            real_part = left_re * right_re + left_im * right_im
            imag_part = left_re * right_im - left_im * right_re
        else:
            real_part = left_re * right_re - left_im * right_im
            imag_part = left_re * right_im + left_im * right_re
        return (jnp.concatenate([real_part, imag_part], axis=-1) * factor).astype(jnp.bfloat16)

    kernel_scale = 1.0 / math.sqrt(seq_len)
    input_spectrum = spectrum(inputs)
    kernel_spectrum = spectrum(filter_taps) * kernel_scale
    outputs = invert(product(kernel_spectrum, input_spectrum, False, 1.0))
    grad_spectrum = spectrum(grad_out)
    grad_inputs = invert(product(kernel_spectrum, grad_spectrum, True, 1.0))
    grad_taps = invert(product(input_spectrum, grad_spectrum, True, kernel_scale))
    return (outputs, grad_inputs, grad_taps)


RADIX = 8


def exact_tables(blocksize, seq_len, lanes):
    j = np.arange(blocksize)
    mats = []
    for r in range(2):
        ang = (j[:, None] * (2 * j[None, :] + r) % (2 * blocksize)).astype(np.float32)
        ang = ang * np.float32(math.pi / blocksize)
        cos, sin = np.cos(ang), np.sin(ang)
        mats.append(np.block([[cos, -sin], [sin, cos]]))
    inverse = np.stack(mats).astype(ml_dtypes.bfloat16)
    forward = np.ascontiguousarray(np.transpose(inverse, (0, 2, 1)))
    k1 = np.arange(1, RADIX // 2 + 1)[:, None, None]
    n = np.arange(2)[None, :, None]
    ang = ((n * blocksize + j[None, None, :]) * k1).astype(np.float32)
    ang = ang * np.float32(2.0 * math.pi / seq_len)
    shape = (RADIX // 2, 2, blocksize, lanes)
    cos = np.ascontiguousarray(np.broadcast_to(np.cos(ang)[..., None], shape))
    sin = np.ascontiguousarray(np.broadcast_to(np.sin(ang)[..., None], shape))
    return forward, inverse, cos, sin


def fused_kernel(
    x_ref, f_ref, g_ref, fwd_hbm, inv_hbm, cos_hbm, sin_hbm, o0_ref, o1_ref, o2_ref,
    buf, spec, mix, unf, obuf, fwd, inv, tcos, tsin,
    send_sem, recv_sem, own_sem, osend_sem, orecv_sem, oown_sem, table_sem,
):
    block, lanes = buf.shape[2], buf.shape[3]
    wide, narrow = lax.axis_index("wide"), lax.axis_index("narrow")
    half, place = wide // 4, wide % 4
    mine = wide * 2 + narrow
    signals = (x_ref, f_ref, g_ref)
    outs = (o0_ref, o1_ref, o2_ref)
    root = float(np.float32(ml_dtypes.bfloat16(math.cos(math.pi / 4))))

    def peer(dh, dp, dc):
        w = (half + dh) % 2 * 4 + (place + dp) % 4
        return w, (narrow + dc) % 2

    offsets = [(dh, dp, dc) for dh in (1, 0) for dp in (0, 1, 2, 3) for dc in (0, 1)]
    others = [o for o in offsets if o != (0, 0, 0)]

    def where(w, c):
        return {"wide": w, "narrow": c}

    def columns(w, c):
        return pl.ds(pl.multiple_of((w % 4 * 2 + c) * lanes, lanes), lanes)

    tables = [
        pltpu.make_async_copy(a, b, table_sem.at[i])
        for i, (a, b) in enumerate(
            ((cos_hbm, tcos), (sin_hbm, tsin), (fwd_hbm, fwd), (inv_hbm, inv))
        )
    ]

    barrier = pltpu.get_barrier_semaphore()
    for o in others:
        w, c = peer(*o)
        pl.semaphore_signal(
            barrier, inc=1, device_id=where(w, c), device_id_type=pl.DeviceIdType.MESH
        )
    pl.semaphore_wait(barrier, len(others))

    def send(s, i):
        w, c = peer(*others[i])
        return pltpu.make_async_remote_copy(
            src_ref=signals[s].at[:, columns(w, c)],
            dst_ref=buf.at[s, mine],
            send_sem=send_sem.at[s, i],
            recv_sem=recv_sem.at[s, mine],
            device_id=where(w, c),
            device_id_type=pl.DeviceIdType.MESH,
        )

    def arrived(s, i):
        w, c = peer(*others[i])
        b = w * 2 + c
        return pltpu.make_async_remote_copy(
            src_ref=buf.at[s, b],
            dst_ref=buf.at[s, b],
            send_sem=send_sem.at[s, i],
            recv_sem=recv_sem.at[s, b],
            device_id=where(w, c),
            device_id_type=pl.DeviceIdType.MESH,
        )

    def own(s):
        return pltpu.make_async_copy(
            signals[s].at[:, columns(wide, narrow)], buf.at[s, mine], own_sem.at[s]
        )

    def launch(s):
        for i in range(len(others)):
            send(s, i).start()
        own(s).start()

    def collect(s):
        for i in range(len(others)):
            arrived(s, i).wait_recv()
        own(s).wait()

    step = 16

    def forward(s):
        def tile(t, carry):
            rows = pl.ds(pl.multiple_of(t * step, step), step)
            low = pl.ds(pl.multiple_of(t * step + block, step), step)
            halves = []
            for n in range(2):
                a = [buf[s, 2 * i + n, rows, :].astype(jnp.float32) for i in range(RADIX)]
                e = [a[i] + a[i + 4] for i in range(4)]
                d = [a[i] - a[i + 4] for i in range(4)]
                even, odd = e[0] + e[2], e[1] + e[3]
                minus = root * (d[1] - d[3])
                plus = root * (d[1] + d[3])
                raw = [
                    (d[0] + minus, -(d[2] + plus)),
                    (e[0] - e[2], e[3] - e[1]),
                    (d[0] - minus, d[2] - plus),
                    (even - odd, None),
                ]
                got = [(even + odd, None)]
                for k, (re, im) in enumerate(raw):
                    cos, sin = tcos[k, n, rows, :], tsin[k, n, rows, :]
                    if im is None:
                        got.append((re * cos, -(re * sin)))
                    else:
                        got.append((re * cos + im * sin, im * cos - re * sin))
                halves.append(got)
            for k in range(RADIX // 2 + 1):
                cols = slice(k * lanes, (k + 1) * lanes)
                (r0, i0), (r1, i1) = halves[0][k], halves[1][k]
                mix[0, rows, cols] = (r0 + r1).astype(jnp.bfloat16)
                mix[1, rows, cols] = (r0 - r1).astype(jnp.bfloat16)
                if i0 is not None:
                    mix[0, low, cols] = (i0 + i1).astype(jnp.bfloat16)
                    mix[1, low, cols] = (i0 - i1).astype(jnp.bfloat16)
                else:
                    mix[0, low, cols] = jnp.zeros_like(r0, jnp.bfloat16)
                    mix[1, low, cols] = jnp.zeros_like(r0, jnp.bfloat16)
            return carry

        lax.fori_loop(0, block // step, tile, 0)
        multiply(fwd, spec.at[s])

    def multiply(table, result):
        def one(r, carry):
            width = mix.shape[2]
            for first in range(0, width, 256):
                cols = slice(first, min(first + 256, width))
                result[r, :, cols] = jnp.dot(
                    table[r], mix[r, :, cols], preferred_element_type=jnp.float32
                )
            return carry

        lax.fori_loop(0, 2, one, 0)

    def combine(left, right, conjugate):
        def tile(t, carry):
            rows = pl.ds(pl.multiple_of(t * step, step), step)
            low = pl.ds(pl.multiple_of(t * step + block, step), step)
            for r in range(2):
                for k in range(RADIX // 2 + 1):
                    cols = slice(k * lanes, (k + 1) * lanes)
                    lr, li = spec[left, r, rows, cols], spec[left, r, low, cols]
                    rr, ri = spec[right, r, rows, cols], spec[right, r, low, cols]
                    if conjugate:
                        re, im = lr * rr + li * ri, lr * ri - li * rr
                    else:
                        re, im = lr * rr - li * ri, lr * ri + li * rr
                    mix[r, rows, cols] = re.astype(jnp.bfloat16)
                    mix[r, low, cols] = im.astype(jnp.bfloat16)
            return carry

        lax.fori_loop(0, block // step, tile, 0)

    scale = 2.0 ** -18
    side = (1 - 2 * half).astype(jnp.float32) * (2.0 * scale)

    def inverse(o, left, right, conjugate):
        combine(left, right, conjugate)
        multiply(inv, unf)

        def tile(t, carry):
            rows = pl.ds(pl.multiple_of(t * step, step), step)
            low = pl.ds(pl.multiple_of(t * step + block, step), step)
            for n in range(2):
                sign = 1 if n == 0 else -1
                zero = slice(0, lanes)
                parts = [(unf[0, rows, zero] + sign * unf[1, rows, zero]) * scale]
                for k in range(RADIX // 2):
                    cols = slice((k + 1) * lanes, (k + 2) * lanes)
                    re = unf[0, rows, cols] + sign * unf[1, rows, cols]
                    im = unf[0, low, cols] + sign * unf[1, low, cols]
                    cos, sin = tcos[k, n, rows, :], tsin[k, n, rows, :]
                    mre = re * cos - im * sin
                    if k == RADIX // 2 - 1:
                        parts.append(mre * scale)
                    else:
                        factor = 2.0 * scale if k == 1 else side
                        parts.append((mre * factor, (im * cos + re * sin) * factor))
                a, (r1, i1), (r2, i2), (r3, i3), b = parts
                top, bottom = a + b, a - b
                left_, right_ = root * (r1 - r3), root * (i1 + i3)
                values = (
                    top + r2 + (r1 + r3),
                    bottom - i2 + (left_ - right_),
                    top - r2 + (i3 - i1),
                    bottom + i2 - (left_ + right_),
                )
                for u in range(4):
                    obuf[o, 2 * u + n, rows, :] = values[u].astype(jnp.bfloat16)
            return carry

        lax.fori_loop(0, block // step, tile, 0)

    near = [(dp, dc) for dp in range(4) for dc in range(2)][1:]

    def give(o, i):
        w, c = peer(0, *near[i])
        return pltpu.make_async_remote_copy(
            src_ref=obuf.at[o, w % 4 * 2 + c],
            dst_ref=outs[o].at[:, columns(wide, narrow)],
            send_sem=osend_sem.at[o, i],
            recv_sem=orecv_sem.at[o, place * 2 + narrow],
            device_id=where(w, c),
            device_id_type=pl.DeviceIdType.MESH,
        )

    def taken(o, i):
        w, c = peer(0, *near[i])
        return pltpu.make_async_remote_copy(
            src_ref=obuf.at[o, w % 4 * 2 + c],
            dst_ref=outs[o].at[:, columns(w, c)],
            send_sem=osend_sem.at[o, i],
            recv_sem=orecv_sem.at[o, w % 4 * 2 + c],
            device_id=where(w, c),
            device_id_type=pl.DeviceIdType.MESH,
        )

    def keep(o):
        return pltpu.make_async_copy(
            obuf.at[o, place * 2 + narrow],
            outs[o].at[:, columns(wide, narrow)],
            oown_sem.at[o],
        )

    def deliver(o):
        for i in range(len(near)):
            give(o, i).start()
        keep(o).start()

    for s in range(3):
        launch(s)
    for t in tables:
        t.start()
    for t in tables:
        t.wait()
    collect(0)
    forward(0)
    collect(1)
    forward(1)
    inverse(0, 1, 0, False)
    deliver(0)
    collect(2)
    forward(2)
    inverse(1, 1, 2, True)
    deliver(1)
    inverse(2, 0, 2, True)
    deliver(2)
    for s in range(3):
        for i in range(len(others)):
            send(s, i).wait_send()
    for o in range(3):
        for i in range(len(near)):
            give(o, i).wait_send()
            taken(o, i).wait_recv()
        keep(o).wait()


def on_device_fused(inputs, filter_taps, grad_out):
    block, channels = inputs.shape
    lanes = channels // RADIX
    tables = exact_tables(block, RADIX * 2 * block, lanes)
    width = (RADIX // 2 + 1) * lanes
    out = jax.ShapeDtypeStruct(inputs.shape, jnp.bfloat16)
    anywhere = pl.BlockSpec(memory_space=pl.ANY)
    return pl.pallas_call(
        fused_kernel,
        out_shape=(out, out, out),
        in_specs=[anywhere] * 7,
        out_specs=(anywhere,) * 3,
        scratch_shapes=[
            pltpu.VMEM((3, 2 * RADIX, block, lanes), jnp.bfloat16),
            pltpu.VMEM((3, 2, 2 * block, width), jnp.float32),
            pltpu.VMEM((2, 2 * block, width), jnp.bfloat16),
            pltpu.VMEM((2, 2 * block, width), jnp.float32),
            pltpu.VMEM((3, RADIX, block, lanes), jnp.bfloat16),
            pltpu.VMEM((2, 2 * block, 2 * block), jnp.bfloat16),
            pltpu.VMEM((2, 2 * block, 2 * block), jnp.bfloat16),
            pltpu.VMEM((RADIX // 2, 2, block, lanes), jnp.float32),
            pltpu.VMEM((RADIX // 2, 2, block, lanes), jnp.float32),
            pltpu.SemaphoreType.DMA((3, 15)),
            pltpu.SemaphoreType.DMA((3, 16)),
            pltpu.SemaphoreType.DMA((3,)),
            pltpu.SemaphoreType.DMA((3, 7)),
            pltpu.SemaphoreType.DMA((3, 8)),
            pltpu.SemaphoreType.DMA((3,)),
            pltpu.SemaphoreType.DMA((4,)),
        ],
        compiler_params=pltpu.CompilerParams(
            collective_id=0, has_side_effects=True, vmem_limit_bytes=48 * 2**20
        ),
    )(inputs, filter_taps, grad_out, *tables)


def solution(mesh):
    in_specs = (
        P(("groups", "wide", "narrow"), None),
        P(("wide", "narrow"), None),
        P(("groups", "wide", "narrow"), None),
    )
    out_specs = (P(("groups", "wide", "narrow"), None),) * 3
    body = on_device_fused if mesh.shape["wide"] == RADIX else on_device
    return jax.shard_map(
        body, mesh=mesh, in_specs=in_specs, out_specs=out_specs, check_vma=False
    )
```

```python
import math

import jax
import jax.numpy as jnp
import ml_dtypes
import numpy as np
from jax import lax
from jax.experimental import pallas as pl
from jax.experimental.pallas import tpu as pltpu
from jax.sharding import PartitionSpec as P


def partner_2(value, axis, distance):
    mask = 2**distance
    pairs = [(source, source ^ mask) for source in range(lax.axis_size(axis))]
    return lax.ppermute(value, axis, pairs)


def on_device(inputs, filter_taps, grad_out):
    span_count = lax.axis_size("wide")
    blocksize = inputs.shape[0]
    channels = inputs.shape[1]
    shares = channels // span_count
    row_count = span_count * shares
    seq_len = span_count * 2 * blocksize
    parity = lax.axis_index("narrow")
    signed = (1 - 2 * parity).astype(jnp.float32)
    counter = jnp.arange(span_count, dtype=jnp.int32)
    long_angles = (counter[:, None] * counter[None, :] % span_count).astype(jnp.float32) * (
        2.0 * math.pi / span_count
    )
    long_cos = jnp.cos(long_angles)
    long_sin = jnp.sin(long_angles)
    long_forward = jnp.concatenate([long_cos, -long_sin], axis=0).astype(jnp.bfloat16)
    long_inverse = jnp.concatenate([long_cos, -long_sin], axis=1).astype(jnp.bfloat16)
    positions = jnp.arange(blocksize, dtype=jnp.int32)

    def first_section(pieces, twist_cos, twist_sin):
        share_count = pieces.shape[1]
        lane_count = pieces.shape[2]
        flatten = pieces.reshape(span_count, share_count * lane_count)
        mixture = jnp.dot(long_forward, flatten, preferred_element_type=jnp.float32)
        mixture = mixture.reshape(2, span_count, share_count, lane_count)
        real_part = mixture[0] * twist_cos + mixture[1] * twist_sin
        imag_part = mixture[1] * twist_cos - mixture[0] * twist_sin
        return jnp.stack([real_part, imag_part]).astype(jnp.bfloat16)

    def long_back(combined_re, combined_im, twist_cos, twist_sin):
        merged_re = combined_re * twist_cos - combined_im * twist_sin
        merged_im = combined_im * twist_cos + combined_re * twist_sin
        share_count = combined_re.shape[1]
        lane_count = combined_re.shape[2]
        stacked = (
            jnp.stack([merged_re, merged_im])
            .astype(jnp.bfloat16)
            .reshape(2 * span_count, share_count * lane_count)
        )
        summed = jnp.dot(long_inverse, stacked, preferred_element_type=jnp.float32) * (
            1.0 / seq_len
        )
        return summed.astype(jnp.bfloat16).reshape(span_count, share_count, lane_count)

    block_product = positions[:, None] * (2 * positions[None, :] + parity) % (2 * blocksize)
    block_angles = block_product.astype(jnp.float32) * (math.pi / blocksize)
    block_cos = jnp.cos(block_angles)
    block_sin = jnp.sin(block_angles)
    forward_mat = jnp.concatenate(
        [
            jnp.concatenate([block_cos, -block_sin], axis=1),
            jnp.concatenate([block_sin, block_cos], axis=1),
        ],
        axis=0,
    ).astype(jnp.bfloat16)
    cos_turned = jnp.transpose(block_cos)
    sin_turned = jnp.transpose(block_sin)
    inverse_mat = jnp.concatenate(
        [
            jnp.concatenate([cos_turned, sin_turned], axis=1),
            jnp.concatenate([-sin_turned, cos_turned], axis=1),
        ],
        axis=0,
    ).astype(jnp.bfloat16)
    twist_product = (parity * blocksize + positions)[None, None, :] * counter[:, None, None]
    twist_angles = twist_product.astype(jnp.float32) * (2.0 * math.pi / seq_len)
    twist_cos = jnp.cos(twist_angles)
    twist_sin = jnp.sin(twist_angles)

    def section_pairs(pieces):
        return first_section(pieces, twist_cos, twist_sin)

    def spectrum(signal):
        arranged = jnp.transpose(signal).reshape(span_count, shares, blocksize)
        twisted = section_pairs(
            lax.all_to_all(arranged, "wide", split_axis=0, concat_axis=0, tiled=True)
        )
        partner = partner_2(twisted, "narrow", 0)
        paired = (signed * twisted.astype(jnp.float32) + partner.astype(jnp.float32)).astype(
            jnp.bfloat16
        )
        joined = jnp.concatenate(
            [paired[0].reshape(row_count, blocksize), paired[1].reshape(row_count, blocksize)],
            axis=1,
        )
        return jnp.dot(joined, forward_mat, preferred_element_type=jnp.float32)

    def invert(spectrum_in):
        unfolded = jnp.dot(spectrum_in, inverse_mat, preferred_element_type=jnp.float32).astype(
            jnp.bfloat16
        )
        partner = partner_2(unfolded, "narrow", 0)
        combined = signed * unfolded.astype(jnp.float32) + partner.astype(jnp.float32)
        comb_re = combined[:, :blocksize].reshape(span_count, shares, blocksize)
        comb_im = combined[:, blocksize:].reshape(span_count, shares, blocksize)
        arranged = long_back(comb_re, comb_im, twist_cos, twist_sin)
        returned = lax.all_to_all(arranged, "wide", split_axis=0, concat_axis=1, tiled=True)
        return jnp.transpose(returned.reshape(channels, blocksize))

    def product(left_side, right_side, conjugate, factor):
        left_re = left_side[..., :blocksize]
        left_im = left_side[..., blocksize:]
        right_re = right_side[..., :blocksize]
        right_im = right_side[..., blocksize:]
        if conjugate:
            real_part = left_re * right_re + left_im * right_im
            imag_part = left_re * right_im - left_im * right_re
        else:
            real_part = left_re * right_re - left_im * right_im
            imag_part = left_re * right_im + left_im * right_re
        return (jnp.concatenate([real_part, imag_part], axis=-1) * factor).astype(jnp.bfloat16)

    kernel_scale = 1.0 / math.sqrt(seq_len)
    input_spectrum = spectrum(inputs)
    kernel_spectrum = spectrum(filter_taps) * kernel_scale
    outputs = invert(product(kernel_spectrum, input_spectrum, False, 1.0))
    grad_spectrum = spectrum(grad_out)
    grad_inputs = invert(product(kernel_spectrum, grad_spectrum, True, 1.0))
    grad_taps = invert(product(input_spectrum, grad_spectrum, True, kernel_scale))
    return (outputs, grad_inputs, grad_taps)


RADIX = 8


def exact_tables(blocksize, seq_len, lanes):
    j = np.arange(blocksize)
    mats = []
    for r in range(2):
        ang = (j[:, None] * (2 * j[None, :] + r) % (2 * blocksize)).astype(np.float32)
        ang = ang * np.float32(math.pi / blocksize)
        cos, sin = np.cos(ang), np.sin(ang)
        mats.append(np.block([[cos, -sin], [sin, cos]]))
    inverse = np.stack(mats).astype(ml_dtypes.bfloat16)
    forward = np.ascontiguousarray(np.transpose(inverse, (0, 2, 1)))
    k1 = np.arange(1, RADIX // 2 + 1)[:, None, None]
    n = np.arange(2)[None, :, None]
    ang = ((n * blocksize + j[None, None, :]) * k1).astype(np.float32)
    ang = ang * np.float32(2.0 * math.pi / seq_len)
    shape = (RADIX // 2, 2, blocksize, lanes)
    cos = np.ascontiguousarray(np.broadcast_to(np.cos(ang)[..., None], shape))
    sin = np.ascontiguousarray(np.broadcast_to(np.sin(ang)[..., None], shape))
    return forward, inverse, cos, sin


def fused_kernel(
    x_ref, f_ref, g_ref, fwd_hbm, inv_hbm, cos_hbm, sin_hbm, o0_ref, o1_ref, o2_ref,
    buf, spec, mix, unf, obuf, fwd, inv, tcos, tsin,
    send_sem, recv_sem, own_sem, osend_sem, orecv_sem, oown_sem, table_sem,
    relay_send_sem, relay_recv_sem,
):
    block, lanes = buf.shape[2], buf.shape[3]
    wide, narrow = lax.axis_index("wide"), lax.axis_index("narrow")
    half, place = wide // 4, wide % 4
    group = lax.axis_index("groups")
    mine = wide * 2 + narrow
    signals = (x_ref, f_ref, g_ref)
    outs = (o0_ref, o1_ref, o2_ref)
    root = float(np.float32(ml_dtypes.bfloat16(math.cos(math.pi / 4))))

    def peer(dh, dp, dc):
        w = (half + dh) % 2 * 4 + (place + dp) % 4
        return w, (narrow + dc) % 2

    offsets = [(dh, dp, dc) for dh in (1, 0) for dp in (0, 1, 2, 3) for dc in (0, 1)]
    others = [o for o in offsets if o != (0, 0, 0)]

    def where(w, c):
        return {"wide": w, "narrow": c}

    def columns(w, c):
        return pl.ds(pl.multiple_of((w % 4 * 2 + c) * lanes, lanes), lanes)

    tables = [
        pltpu.make_async_copy(a, b, table_sem.at[i])
        for i, (a, b) in enumerate(
            ((cos_hbm, tcos), (sin_hbm, tsin), (fwd_hbm, fwd), (inv_hbm, inv))
        )
    ]

    barrier = pltpu.get_barrier_semaphore()
    for o in others:
        w, c = peer(*o)
        pl.semaphore_signal(
            barrier, inc=1, device_id=where(w, c), device_id_type=pl.DeviceIdType.MESH
        )
    pl.semaphore_signal(
        barrier, inc=1, device_id={"groups": 1 - group}, device_id_type=pl.DeviceIdType.MESH
    )
    pl.semaphore_wait(barrier, len(others) + 1)

    far = [i for i, o in enumerate(others) if o[0] == 1]

    def share(g):
        return pl.ds(pl.multiple_of(g * (block // 2), block // 2), block // 2)

    def piece(ref, s, i, g):
        return ref.at[share(g)] if s == 1 and i in far else ref

    def send(s, i):
        w, c = peer(*others[i])
        return pltpu.make_async_remote_copy(
            src_ref=piece(signals[s].at[:, columns(w, c)], s, i, group),
            dst_ref=piece(buf.at[s, mine], s, i, group),
            send_sem=send_sem.at[s, i],
            recv_sem=recv_sem.at[s, mine],
            device_id=where(w, c),
            device_id_type=pl.DeviceIdType.MESH,
        )

    def arrived(s, i):
        w, c = peer(*others[i])
        b = w * 2 + c
        return pltpu.make_async_remote_copy(
            src_ref=piece(buf.at[s, b], s, i, group),
            dst_ref=piece(buf.at[s, b], s, i, group),
            send_sem=send_sem.at[s, i],
            recv_sem=recv_sem.at[s, b],
            device_id=where(w, c),
            device_id_type=pl.DeviceIdType.MESH,
        )

    def relay(i, g):
        w, c = peer(*others[i])
        rows = piece(buf.at[1, w * 2 + c], 1, i, g)
        return pltpu.make_async_remote_copy(
            src_ref=rows,
            dst_ref=rows,
            send_sem=relay_send_sem.at[i],
            recv_sem=relay_recv_sem.at[i],
            device_id={"groups": 1 - group},
            device_id_type=pl.DeviceIdType.MESH,
        )

    def own(s):
        return pltpu.make_async_copy(
            signals[s].at[:, columns(wide, narrow)], buf.at[s, mine], own_sem.at[s]
        )

    def launch(s):
        for i in range(len(others)):
            send(s, i).start()
        own(s).start()

    def collect(s):
        for i in range(len(others)):
            arrived(s, i).wait_recv()
            if s == 1 and i in far:
                relay(i, group).start()
        if s == 1:
            for i in far:
                relay(i, 1 - group).wait_recv()
        own(s).wait()

    step = 16

    def forward(s):
        def tile(t, carry):
            rows = pl.ds(pl.multiple_of(t * step, step), step)
            low = pl.ds(pl.multiple_of(t * step + block, step), step)
            halves = []
            for n in range(2):
                a = [buf[s, 2 * i + n, rows, :].astype(jnp.float32) for i in range(RADIX)]
                e = [a[i] + a[i + 4] for i in range(4)]
                d = [a[i] - a[i + 4] for i in range(4)]
                even, odd = e[0] + e[2], e[1] + e[3]
                minus = root * (d[1] - d[3])
                plus = root * (d[1] + d[3])
                raw = [
                    (d[0] + minus, -(d[2] + plus)),
                    (e[0] - e[2], e[3] - e[1]),
                    (d[0] - minus, d[2] - plus),
                    (even - odd, None),
                ]
                got = [(even + odd, None)]
                for k, (re, im) in enumerate(raw):
                    cos, sin = tcos[k, n, rows, :], tsin[k, n, rows, :]
                    if im is None:
                        got.append((re * cos, -(re * sin)))
                    else:
                        got.append((re * cos + im * sin, im * cos - re * sin))
                halves.append(got)
            for k in range(RADIX // 2 + 1):
                cols = slice(k * lanes, (k + 1) * lanes)
                (r0, i0), (r1, i1) = halves[0][k], halves[1][k]
                mix[0, rows, cols] = (r0 + r1).astype(jnp.bfloat16)
                mix[1, rows, cols] = (r0 - r1).astype(jnp.bfloat16)
                if i0 is not None:
                    mix[0, low, cols] = (i0 + i1).astype(jnp.bfloat16)
                    mix[1, low, cols] = (i0 - i1).astype(jnp.bfloat16)
                else:
                    mix[0, low, cols] = jnp.zeros_like(r0, jnp.bfloat16)
                    mix[1, low, cols] = jnp.zeros_like(r0, jnp.bfloat16)
            return carry

        lax.fori_loop(0, block // step, tile, 0)
        multiply(fwd, spec.at[s])

    def multiply(table, result):
        def one(r, carry):
            width = mix.shape[2]
            for first in range(0, width, 256):
                cols = slice(first, min(first + 256, width))
                result[r, :, cols] = jnp.dot(
                    table[r], mix[r, :, cols], preferred_element_type=jnp.float32
                )
            return carry

        lax.fori_loop(0, 2, one, 0)

    def combine(left, right, conjugate):
        def tile(t, carry):
            rows = pl.ds(pl.multiple_of(t * step, step), step)
            low = pl.ds(pl.multiple_of(t * step + block, step), step)
            for r in range(2):
                for k in range(RADIX // 2 + 1):
                    cols = slice(k * lanes, (k + 1) * lanes)
                    lr, li = spec[left, r, rows, cols], spec[left, r, low, cols]
                    rr, ri = spec[right, r, rows, cols], spec[right, r, low, cols]
                    if conjugate:
                        re, im = lr * rr + li * ri, lr * ri - li * rr
                    else:
                        re, im = lr * rr - li * ri, lr * ri + li * rr
                    mix[r, rows, cols] = re.astype(jnp.bfloat16)
                    mix[r, low, cols] = im.astype(jnp.bfloat16)
            return carry

        lax.fori_loop(0, block // step, tile, 0)

    scale = 2.0 ** -18
    side = (1 - 2 * half).astype(jnp.float32) * (2.0 * scale)

    def inverse(o, left, right, conjugate):
        combine(left, right, conjugate)
        multiply(inv, unf)

        def tile(t, carry):
            rows = pl.ds(pl.multiple_of(t * step, step), step)
            low = pl.ds(pl.multiple_of(t * step + block, step), step)
            for n in range(2):
                sign = 1 if n == 0 else -1
                zero = slice(0, lanes)
                parts = [(unf[0, rows, zero] + sign * unf[1, rows, zero]) * scale]
                for k in range(RADIX // 2):
                    cols = slice((k + 1) * lanes, (k + 2) * lanes)
                    re = unf[0, rows, cols] + sign * unf[1, rows, cols]
                    im = unf[0, low, cols] + sign * unf[1, low, cols]
                    cos, sin = tcos[k, n, rows, :], tsin[k, n, rows, :]
                    mre = re * cos - im * sin
                    if k == RADIX // 2 - 1:
                        parts.append(mre * scale)
                    else:
                        factor = 2.0 * scale if k == 1 else side
                        parts.append((mre * factor, (im * cos + re * sin) * factor))
                a, (r1, i1), (r2, i2), (r3, i3), b = parts
                top, bottom = a + b, a - b
                left_, right_ = root * (r1 - r3), root * (i1 + i3)
                values = (
                    top + r2 + (r1 + r3),
                    bottom - i2 + (left_ - right_),
                    top - r2 + (i3 - i1),
                    bottom + i2 - (left_ + right_),
                )
                for u in range(4):
                    obuf[o, 2 * u + n, rows, :] = values[u].astype(jnp.bfloat16)
            return carry

        lax.fori_loop(0, block // step, tile, 0)

    near = [(dp, dc) for dp in range(4) for dc in range(2)][1:]

    def give(o, i):
        w, c = peer(0, *near[i])
        return pltpu.make_async_remote_copy(
            src_ref=obuf.at[o, w % 4 * 2 + c],
            dst_ref=outs[o].at[:, columns(wide, narrow)],
            send_sem=osend_sem.at[o, i],
            recv_sem=orecv_sem.at[o, place * 2 + narrow],
            device_id=where(w, c),
            device_id_type=pl.DeviceIdType.MESH,
        )

    def taken(o, i):
        w, c = peer(0, *near[i])
        return pltpu.make_async_remote_copy(
            src_ref=obuf.at[o, w % 4 * 2 + c],
            dst_ref=outs[o].at[:, columns(w, c)],
            send_sem=osend_sem.at[o, i],
            recv_sem=orecv_sem.at[o, w % 4 * 2 + c],
            device_id=where(w, c),
            device_id_type=pl.DeviceIdType.MESH,
        )

    def keep(o):
        return pltpu.make_async_copy(
            obuf.at[o, place * 2 + narrow],
            outs[o].at[:, columns(wide, narrow)],
            oown_sem.at[o],
        )

    def deliver(o):
        for i in range(len(near)):
            give(o, i).start()
        keep(o).start()

    launch(1)
    launch(0)
    launch(2)
    for t in tables:
        t.start()
    for t in tables:
        t.wait()
    collect(1)
    forward(1)
    collect(0)
    forward(0)
    inverse(0, 1, 0, False)
    deliver(0)
    collect(2)
    forward(2)
    inverse(1, 1, 2, True)
    deliver(1)
    inverse(2, 0, 2, True)
    deliver(2)
    for i in far:
        relay(i, group).wait_send()
    for s in range(3):
        for i in range(len(others)):
            send(s, i).wait_send()
    for o in range(3):
        for i in range(len(near)):
            give(o, i).wait_send()
            taken(o, i).wait_recv()
        keep(o).wait()


def on_device_fused(inputs, filter_taps, grad_out):
    block, channels = inputs.shape
    lanes = channels // RADIX
    tables = exact_tables(block, RADIX * 2 * block, lanes)
    width = (RADIX // 2 + 1) * lanes
    out = jax.ShapeDtypeStruct(inputs.shape, jnp.bfloat16)
    anywhere = pl.BlockSpec(memory_space=pltpu.HBM)
    return pl.pallas_call(
        fused_kernel,
        out_shape=(out, out, out),
        in_specs=[anywhere] * 7,
        out_specs=(anywhere,) * 3,
        scratch_shapes=[
            pltpu.VMEM((3, 2 * RADIX, block, lanes), jnp.bfloat16),
            pltpu.VMEM((3, 2, 2 * block, width), jnp.float32),
            pltpu.VMEM((2, 2 * block, width), jnp.bfloat16),
            pltpu.VMEM((2, 2 * block, width), jnp.float32),
            pltpu.VMEM((3, RADIX, block, lanes), jnp.bfloat16),
            pltpu.VMEM((2, 2 * block, 2 * block), jnp.bfloat16),
            pltpu.VMEM((2, 2 * block, 2 * block), jnp.bfloat16),
            pltpu.VMEM((RADIX // 2, 2, block, lanes), jnp.float32),
            pltpu.VMEM((RADIX // 2, 2, block, lanes), jnp.float32),
            pltpu.SemaphoreType.DMA((3, 15)),
            pltpu.SemaphoreType.DMA((3, 16)),
            pltpu.SemaphoreType.DMA((3,)),
            pltpu.SemaphoreType.DMA((3, 7)),
            pltpu.SemaphoreType.DMA((3, 8)),
            pltpu.SemaphoreType.DMA((3,)),
            pltpu.SemaphoreType.DMA((4,)),
            pltpu.SemaphoreType.DMA((8,)),
            pltpu.SemaphoreType.DMA((8,)),
        ],
        compiler_params=pltpu.CompilerParams(
            collective_id=0, has_side_effects=True, vmem_limit_bytes=48 * 2**20
        ),
    )(inputs, filter_taps, grad_out, *tables)


def solution(mesh):
    in_specs = (
        P(("groups", "wide", "narrow"), None),
        P(("wide", "narrow"), None),
        P(("groups", "wide", "narrow"), None),
    )
    out_specs = (P(("groups", "wide", "narrow"), None),) * 3
    body = on_device_fused if (mesh.shape["wide"], mesh.shape["groups"]) == (RADIX, 2) else on_device
    return jax.shard_map(
        body, mesh=mesh, in_specs=in_specs, out_specs=out_specs, check_vma=False
    )
```

```python
import math

import jax
import jax.numpy as jnp
import ml_dtypes
import numpy as np
from jax import lax
from jax.experimental import pallas as pl
from jax.experimental.pallas import tpu as pltpu
from jax.sharding import PartitionSpec as P


def partner_2(value, axis, distance):
    mask = 2**distance
    pairs = [(source, source ^ mask) for source in range(lax.axis_size(axis))]
    return lax.ppermute(value, axis, pairs)


def on_device(inputs, filter_taps, grad_out):
    span_count = lax.axis_size("wide")
    blocksize = inputs.shape[0]
    channels = inputs.shape[1]
    shares = channels // span_count
    row_count = span_count * shares
    seq_len = span_count * 2 * blocksize
    parity = lax.axis_index("narrow")
    signed = (1 - 2 * parity).astype(jnp.float32)
    counter = jnp.arange(span_count, dtype=jnp.int32)
    long_angles = (counter[:, None] * counter[None, :] % span_count).astype(jnp.float32) * (
        2.0 * math.pi / span_count
    )
    long_cos = jnp.cos(long_angles)
    long_sin = jnp.sin(long_angles)
    long_forward = jnp.concatenate([long_cos, -long_sin], axis=0).astype(jnp.bfloat16)
    long_inverse = jnp.concatenate([long_cos, -long_sin], axis=1).astype(jnp.bfloat16)
    positions = jnp.arange(blocksize, dtype=jnp.int32)

    def first_section(pieces, twist_cos, twist_sin):
        share_count = pieces.shape[1]
        lane_count = pieces.shape[2]
        flatten = pieces.reshape(span_count, share_count * lane_count)
        mixture = jnp.dot(long_forward, flatten, preferred_element_type=jnp.float32)
        mixture = mixture.reshape(2, span_count, share_count, lane_count)
        real_part = mixture[0] * twist_cos + mixture[1] * twist_sin
        imag_part = mixture[1] * twist_cos - mixture[0] * twist_sin
        return jnp.stack([real_part, imag_part]).astype(jnp.bfloat16)

    def long_back(combined_re, combined_im, twist_cos, twist_sin):
        merged_re = combined_re * twist_cos - combined_im * twist_sin
        merged_im = combined_im * twist_cos + combined_re * twist_sin
        share_count = combined_re.shape[1]
        lane_count = combined_re.shape[2]
        stacked = (
            jnp.stack([merged_re, merged_im])
            .astype(jnp.bfloat16)
            .reshape(2 * span_count, share_count * lane_count)
        )
        summed = jnp.dot(long_inverse, stacked, preferred_element_type=jnp.float32) * (
            1.0 / seq_len
        )
        return summed.astype(jnp.bfloat16).reshape(span_count, share_count, lane_count)

    block_product = positions[:, None] * (2 * positions[None, :] + parity) % (2 * blocksize)
    block_angles = block_product.astype(jnp.float32) * (math.pi / blocksize)
    block_cos = jnp.cos(block_angles)
    block_sin = jnp.sin(block_angles)
    forward_mat = jnp.concatenate(
        [
            jnp.concatenate([block_cos, -block_sin], axis=1),
            jnp.concatenate([block_sin, block_cos], axis=1),
        ],
        axis=0,
    ).astype(jnp.bfloat16)
    cos_turned = jnp.transpose(block_cos)
    sin_turned = jnp.transpose(block_sin)
    inverse_mat = jnp.concatenate(
        [
            jnp.concatenate([cos_turned, sin_turned], axis=1),
            jnp.concatenate([-sin_turned, cos_turned], axis=1),
        ],
        axis=0,
    ).astype(jnp.bfloat16)
    twist_product = (parity * blocksize + positions)[None, None, :] * counter[:, None, None]
    twist_angles = twist_product.astype(jnp.float32) * (2.0 * math.pi / seq_len)
    twist_cos = jnp.cos(twist_angles)
    twist_sin = jnp.sin(twist_angles)

    def section_pairs(pieces):
        return first_section(pieces, twist_cos, twist_sin)

    def spectrum(signal):
        arranged = jnp.transpose(signal).reshape(span_count, shares, blocksize)
        twisted = section_pairs(
            lax.all_to_all(arranged, "wide", split_axis=0, concat_axis=0, tiled=True)
        )
        partner = partner_2(twisted, "narrow", 0)
        paired = (signed * twisted.astype(jnp.float32) + partner.astype(jnp.float32)).astype(
            jnp.bfloat16
        )
        joined = jnp.concatenate(
            [paired[0].reshape(row_count, blocksize), paired[1].reshape(row_count, blocksize)],
            axis=1,
        )
        return jnp.dot(joined, forward_mat, preferred_element_type=jnp.float32)

    def invert(spectrum_in):
        unfolded = jnp.dot(spectrum_in, inverse_mat, preferred_element_type=jnp.float32).astype(
            jnp.bfloat16
        )
        partner = partner_2(unfolded, "narrow", 0)
        combined = signed * unfolded.astype(jnp.float32) + partner.astype(jnp.float32)
        comb_re = combined[:, :blocksize].reshape(span_count, shares, blocksize)
        comb_im = combined[:, blocksize:].reshape(span_count, shares, blocksize)
        arranged = long_back(comb_re, comb_im, twist_cos, twist_sin)
        returned = lax.all_to_all(arranged, "wide", split_axis=0, concat_axis=1, tiled=True)
        return jnp.transpose(returned.reshape(channels, blocksize))

    def product(left_side, right_side, conjugate, factor):
        left_re = left_side[..., :blocksize]
        left_im = left_side[..., blocksize:]
        right_re = right_side[..., :blocksize]
        right_im = right_side[..., blocksize:]
        if conjugate:
            real_part = left_re * right_re + left_im * right_im
            imag_part = left_re * right_im - left_im * right_re
        else:
            real_part = left_re * right_re - left_im * right_im
            imag_part = left_re * right_im + left_im * right_re
        return (jnp.concatenate([real_part, imag_part], axis=-1) * factor).astype(jnp.bfloat16)

    kernel_scale = 1.0 / math.sqrt(seq_len)
    input_spectrum = spectrum(inputs)
    kernel_spectrum = spectrum(filter_taps) * kernel_scale
    outputs = invert(product(kernel_spectrum, input_spectrum, False, 1.0))
    grad_spectrum = spectrum(grad_out)
    grad_inputs = invert(product(kernel_spectrum, grad_spectrum, True, 1.0))
    grad_taps = invert(product(input_spectrum, grad_spectrum, True, kernel_scale))
    return (outputs, grad_inputs, grad_taps)


RADIX = 8


def exact_tables(blocksize, seq_len, lanes):
    j = np.arange(blocksize)
    mats = []
    for r in range(2):
        ang = (j[:, None] * (2 * j[None, :] + r) % (2 * blocksize)).astype(np.float32)
        ang = ang * np.float32(math.pi / blocksize)
        cos, sin = np.cos(ang), np.sin(ang)
        mats.append(np.block([[cos, -sin], [sin, cos]]))
    inverse = np.stack(mats).astype(ml_dtypes.bfloat16)
    forward = np.ascontiguousarray(np.transpose(inverse, (0, 2, 1)))
    k1 = np.arange(1, RADIX // 2 + 1)[:, None, None]
    n = np.arange(2)[None, :, None]
    ang = ((n * blocksize + j[None, None, :]) * k1).astype(np.float32)
    ang = ang * np.float32(2.0 * math.pi / seq_len)
    shape = (RADIX // 2, 2, blocksize, lanes)
    cos = np.ascontiguousarray(np.broadcast_to(np.cos(ang)[..., None], shape))
    sin = np.ascontiguousarray(np.broadcast_to(np.sin(ang)[..., None], shape))
    return forward, inverse, cos, sin


def fused_kernel(
    x_ref, f_ref, g_ref, fwd_hbm, inv_hbm, cos_hbm, sin_hbm, o0_ref, o1_ref, o2_ref,
    buf, spec, mix, unf, obuf, fwd, inv, tcos, tsin,
    send_sem, recv_sem, own_sem, osend_sem, orecv_sem, oown_sem, table_sem,
    relay_send_sem, relay_recv_sem,
):
    block, lanes = buf.shape[2], buf.shape[3]
    wide, narrow = lax.axis_index("wide"), lax.axis_index("narrow")
    half, place = wide // 4, wide % 4
    group = lax.axis_index("groups")
    mine = wide * 2 + narrow
    signals = (x_ref, f_ref, g_ref)
    outs = (o0_ref, o1_ref, o2_ref)
    root = float(np.float32(ml_dtypes.bfloat16(math.cos(math.pi / 4))))

    def peer(dh, dp, dc):
        w = (half + dh) % 2 * 4 + (place + dp) % 4
        return w, (narrow + dc) % 2

    offsets = [(dh, dp, dc) for dh in (1, 0) for dp in (0, 1, 2, 3) for dc in (0, 1)]
    others = [o for o in offsets if o != (0, 0, 0)]

    def where(w, c):
        return {"wide": w, "narrow": c}

    def columns(w, c):
        return pl.ds(pl.multiple_of((w % 4 * 2 + c) * lanes, lanes), lanes)

    tables = [
        pltpu.make_async_copy(a, b, table_sem.at[i])
        for i, (a, b) in enumerate(
            ((cos_hbm, tcos), (sin_hbm, tsin), (fwd_hbm, fwd), (inv_hbm, inv))
        )
    ]

    barrier = pltpu.get_barrier_semaphore()
    for o in others:
        w, c = peer(*o)
        pl.semaphore_signal(
            barrier, inc=1, device_id=where(w, c), device_id_type=pl.DeviceIdType.MESH
        )
    pl.semaphore_signal(
        barrier, inc=1, device_id={"groups": 1 - group}, device_id_type=pl.DeviceIdType.MESH
    )
    pl.semaphore_wait(barrier, len(others) + 1)

    far = [i for i, o in enumerate(others) if o[0] == 1]

    def share(g):
        return pl.ds(pl.multiple_of(g * (block // 2), block // 2), block // 2)

    def piece(ref, s, i, g):
        return ref.at[share(g)] if s == 1 and i in far else ref

    def send(s, i):
        w, c = peer(*others[i])
        return pltpu.make_async_remote_copy(
            src_ref=piece(signals[s].at[:, columns(w, c)], s, i, group),
            dst_ref=piece(buf.at[s, mine], s, i, group),
            send_sem=send_sem.at[s, i],
            recv_sem=recv_sem.at[s, mine],
            device_id=where(w, c),
            device_id_type=pl.DeviceIdType.MESH,
        )

    def arrived(s, i):
        w, c = peer(*others[i])
        b = w * 2 + c
        return pltpu.make_async_remote_copy(
            src_ref=piece(buf.at[s, b], s, i, group),
            dst_ref=piece(buf.at[s, b], s, i, group),
            send_sem=send_sem.at[s, i],
            recv_sem=recv_sem.at[s, b],
            device_id=where(w, c),
            device_id_type=pl.DeviceIdType.MESH,
        )

    def relay(i, g):
        w, c = peer(*others[i])
        rows = piece(buf.at[1, w * 2 + c], 1, i, g)
        return pltpu.make_async_remote_copy(
            src_ref=rows,
            dst_ref=rows,
            send_sem=relay_send_sem.at[i],
            recv_sem=relay_recv_sem.at[i],
            device_id={"groups": 1 - group},
            device_id_type=pl.DeviceIdType.MESH,
        )

    def own(s):
        return pltpu.make_async_copy(
            signals[s].at[:, columns(wide, narrow)], buf.at[s, mine], own_sem.at[s]
        )

    def launch(s):
        for i in reversed(range(len(others))):
            send(s, i).start()
        own(s).start()

    def collect(s):
        for i in range(len(others)):
            arrived(s, i).wait_recv()
            if s == 1 and i in far:
                relay(i, group).start()
        if s == 1:
            for i in far:
                relay(i, 1 - group).wait_recv()
        own(s).wait()

    step = 16

    def forward(s):
        def tile(t, carry):
            rows = pl.ds(pl.multiple_of(t * step, step), step)
            low = pl.ds(pl.multiple_of(t * step + block, step), step)
            halves = []
            for n in range(2):
                a = [buf[s, 2 * i + n, rows, :].astype(jnp.float32) for i in range(RADIX)]
                e = [a[i] + a[i + 4] for i in range(4)]
                d = [a[i] - a[i + 4] for i in range(4)]
                even, odd = e[0] + e[2], e[1] + e[3]
                minus = root * (d[1] - d[3])
                plus = root * (d[1] + d[3])
                raw = [
                    (d[0] + minus, -(d[2] + plus)),
                    (e[0] - e[2], e[3] - e[1]),
                    (d[0] - minus, d[2] - plus),
                    (even - odd, None),
                ]
                got = [(even + odd, None)]
                for k, (re, im) in enumerate(raw):
                    cos, sin = tcos[k, n, rows, :], tsin[k, n, rows, :]
                    if im is None:
                        got.append((re * cos, -(re * sin)))
                    else:
                        got.append((re * cos + im * sin, im * cos - re * sin))
                halves.append(got)
            for k in range(RADIX // 2 + 1):
                cols = slice(k * lanes, (k + 1) * lanes)
                (r0, i0), (r1, i1) = halves[0][k], halves[1][k]
                mix[0, rows, cols] = (r0 + r1).astype(jnp.bfloat16)
                mix[1, rows, cols] = (r0 - r1).astype(jnp.bfloat16)
                if i0 is not None:
                    mix[0, low, cols] = (i0 + i1).astype(jnp.bfloat16)
                    mix[1, low, cols] = (i0 - i1).astype(jnp.bfloat16)
                else:
                    mix[0, low, cols] = jnp.zeros_like(r0, jnp.bfloat16)
                    mix[1, low, cols] = jnp.zeros_like(r0, jnp.bfloat16)
            return carry

        lax.fori_loop(0, block // step, tile, 0)
        multiply(fwd, spec.at[s])

    def multiply(table, result):
        def one(r, carry):
            width = mix.shape[2]
            for first in range(0, width, 256):
                cols = slice(first, min(first + 256, width))
                result[r, :, cols] = jnp.dot(
                    table[r], mix[r, :, cols], preferred_element_type=jnp.float32
                )
            return carry

        lax.fori_loop(0, 2, one, 0)

    def combine(left, right, conjugate):
        def tile(t, carry):
            rows = pl.ds(pl.multiple_of(t * step, step), step)
            low = pl.ds(pl.multiple_of(t * step + block, step), step)
            for r in range(2):
                for k in range(RADIX // 2 + 1):
                    cols = slice(k * lanes, (k + 1) * lanes)
                    lr, li = spec[left, r, rows, cols], spec[left, r, low, cols]
                    rr, ri = spec[right, r, rows, cols], spec[right, r, low, cols]
                    if conjugate:
                        re, im = lr * rr + li * ri, lr * ri - li * rr
                    else:
                        re, im = lr * rr - li * ri, lr * ri + li * rr
                    mix[r, rows, cols] = re.astype(jnp.bfloat16)
                    mix[r, low, cols] = im.astype(jnp.bfloat16)
            return carry

        lax.fori_loop(0, block // step, tile, 0)

    scale = 2.0 ** -18
    side = (1 - 2 * half).astype(jnp.float32) * (2.0 * scale)

    def inverse(o, left, right, conjugate):
        combine(left, right, conjugate)
        multiply(inv, unf)

        def tile(t, carry):
            rows = pl.ds(pl.multiple_of(t * step, step), step)
            low = pl.ds(pl.multiple_of(t * step + block, step), step)
            for n in range(2):
                sign = 1 if n == 0 else -1
                zero = slice(0, lanes)
                parts = [(unf[0, rows, zero] + sign * unf[1, rows, zero]) * scale]
                for k in range(RADIX // 2):
                    cols = slice((k + 1) * lanes, (k + 2) * lanes)
                    re = unf[0, rows, cols] + sign * unf[1, rows, cols]
                    im = unf[0, low, cols] + sign * unf[1, low, cols]
                    cos, sin = tcos[k, n, rows, :], tsin[k, n, rows, :]
                    mre = re * cos - im * sin
                    if k == RADIX // 2 - 1:
                        parts.append(mre * scale)
                    else:
                        factor = 2.0 * scale if k == 1 else side
                        parts.append((mre * factor, (im * cos + re * sin) * factor))
                a, (r1, i1), (r2, i2), (r3, i3), b = parts
                top, bottom = a + b, a - b
                left_, right_ = root * (r1 - r3), root * (i1 + i3)
                values = (
                    top + r2 + (r1 + r3),
                    bottom - i2 + (left_ - right_),
                    top - r2 + (i3 - i1),
                    bottom + i2 - (left_ + right_),
                )
                for u in range(4):
                    obuf[o, 2 * u + n, rows, :] = values[u].astype(jnp.bfloat16)
            return carry

        lax.fori_loop(0, block // step, tile, 0)

    near = [(dp, dc) for dp in range(4) for dc in range(2)][1:]

    def give(o, i):
        w, c = peer(0, *near[i])
        return pltpu.make_async_remote_copy(
            src_ref=obuf.at[o, w % 4 * 2 + c],
            dst_ref=outs[o].at[:, columns(wide, narrow)],
            send_sem=osend_sem.at[o, i],
            recv_sem=orecv_sem.at[o, place * 2 + narrow],
            device_id=where(w, c),
            device_id_type=pl.DeviceIdType.MESH,
        )

    def taken(o, i):
        w, c = peer(0, *near[i])
        return pltpu.make_async_remote_copy(
            src_ref=obuf.at[o, w % 4 * 2 + c],
            dst_ref=outs[o].at[:, columns(w, c)],
            send_sem=osend_sem.at[o, i],
            recv_sem=orecv_sem.at[o, w % 4 * 2 + c],
            device_id=where(w, c),
            device_id_type=pl.DeviceIdType.MESH,
        )

    def keep(o):
        return pltpu.make_async_copy(
            obuf.at[o, place * 2 + narrow],
            outs[o].at[:, columns(wide, narrow)],
            oown_sem.at[o],
        )

    def deliver(o):
        for i in range(len(near)):
            give(o, i).start()
        keep(o).start()

    launch(1)
    launch(0)
    launch(2)
    for t in tables:
        t.start()
    for t in tables:
        t.wait()
    collect(1)
    forward(1)
    collect(0)
    forward(0)
    inverse(0, 1, 0, False)
    deliver(0)
    collect(2)
    forward(2)
    inverse(1, 1, 2, True)
    deliver(1)
    inverse(2, 0, 2, True)
    deliver(2)
    for i in far:
        relay(i, group).wait_send()
    for s in range(3):
        for i in range(len(others)):
            send(s, i).wait_send()
    for o in range(3):
        for i in range(len(near)):
            give(o, i).wait_send()
            taken(o, i).wait_recv()
        keep(o).wait()


def settle_kernel(a0, a1, a2, o0, o1, o2, held, load_sem, store_sem):
    pairs = ((a0, o0), (a1, o1), (a2, o2))
    loads = [
        pltpu.make_async_copy(a, held.at[i], load_sem.at[i]) for i, (a, _) in enumerate(pairs)
    ]
    stores = [
        pltpu.make_async_copy(held.at[i], o, store_sem.at[i]) for i, (_, o) in enumerate(pairs)
    ]
    for load in loads:
        load.start()
    for load, store in zip(loads, stores):
        load.wait()
        store.start()
    for store in stores:
        store.wait()


def on_device_fused(inputs, filter_taps, grad_out):
    block, channels = inputs.shape
    lanes = channels // RADIX
    tables = exact_tables(block, RADIX * 2 * block, lanes)
    width = (RADIX // 2 + 1) * lanes
    out = jax.ShapeDtypeStruct(inputs.shape, jnp.bfloat16)
    anywhere = pl.BlockSpec(memory_space=pltpu.HBM)
    results = pl.pallas_call(
        fused_kernel,
        out_shape=(out, out, out),
        in_specs=[anywhere] * 7,
        out_specs=(anywhere,) * 3,
        scratch_shapes=[
            pltpu.VMEM((3, 2 * RADIX, block, lanes), jnp.bfloat16),
            pltpu.VMEM((3, 2, 2 * block, width), jnp.float32),
            pltpu.VMEM((2, 2 * block, width), jnp.bfloat16),
            pltpu.VMEM((2, 2 * block, width), jnp.float32),
            pltpu.VMEM((3, RADIX, block, lanes), jnp.bfloat16),
            pltpu.VMEM((2, 2 * block, 2 * block), jnp.bfloat16),
            pltpu.VMEM((2, 2 * block, 2 * block), jnp.bfloat16),
            pltpu.VMEM((RADIX // 2, 2, block, lanes), jnp.float32),
            pltpu.VMEM((RADIX // 2, 2, block, lanes), jnp.float32),
            pltpu.SemaphoreType.DMA((3, 15)),
            pltpu.SemaphoreType.DMA((3, 16)),
            pltpu.SemaphoreType.DMA((3,)),
            pltpu.SemaphoreType.DMA((3, 7)),
            pltpu.SemaphoreType.DMA((3, 8)),
            pltpu.SemaphoreType.DMA((3,)),
            pltpu.SemaphoreType.DMA((4,)),
            pltpu.SemaphoreType.DMA((8,)),
            pltpu.SemaphoreType.DMA((8,)),
        ],
        compiler_params=pltpu.CompilerParams(
            collective_id=0, has_side_effects=True, vmem_limit_bytes=60 * 2**20
        ),
    )(inputs, filter_taps, grad_out, *tables)
    return pl.pallas_call(
        settle_kernel,
        out_shape=(out, out, out),
        in_specs=[anywhere] * 3,
        out_specs=(anywhere,) * 3,
        scratch_shapes=[
            pltpu.VMEM((3,) + inputs.shape, jnp.bfloat16),
            pltpu.SemaphoreType.DMA((3,)),
            pltpu.SemaphoreType.DMA((3,)),
        ],
    )(*results)


def solution(mesh):
    in_specs = (
        P(("groups", "wide", "narrow"), None),
        P(("wide", "narrow"), None),
        P(("groups", "wide", "narrow"), None),
    )
    out_specs = (P(("groups", "wide", "narrow"), None),) * 3
    body = on_device_fused if (mesh.shape["wide"], mesh.shape["groups"]) == (RADIX, 2) else on_device
    return jax.shard_map(
        body, mesh=mesh, in_specs=in_specs, out_specs=out_specs, check_vma=False
    )
```

```python
import math

import jax
import jax.numpy as jnp
import ml_dtypes
import numpy as np
from jax import lax
from jax.experimental import pallas as pl
from jax.experimental.pallas import tpu as pltpu
from jax.sharding import PartitionSpec as P


def partner_2(value, axis, distance):
    mask = 2**distance
    pairs = [(source, source ^ mask) for source in range(lax.axis_size(axis))]
    return lax.ppermute(value, axis, pairs)


def on_device(inputs, filter_taps, grad_out):
    span_count = lax.axis_size("wide")
    blocksize = inputs.shape[0]
    channels = inputs.shape[1]
    shares = channels // span_count
    row_count = span_count * shares
    seq_len = span_count * 2 * blocksize
    parity = lax.axis_index("narrow")
    signed = (1 - 2 * parity).astype(jnp.float32)
    counter = jnp.arange(span_count, dtype=jnp.int32)
    long_angles = (counter[:, None] * counter[None, :] % span_count).astype(jnp.float32) * (
        2.0 * math.pi / span_count
    )
    long_cos = jnp.cos(long_angles)
    long_sin = jnp.sin(long_angles)
    long_forward = jnp.concatenate([long_cos, -long_sin], axis=0).astype(jnp.bfloat16)
    long_inverse = jnp.concatenate([long_cos, -long_sin], axis=1).astype(jnp.bfloat16)
    positions = jnp.arange(blocksize, dtype=jnp.int32)

    def first_section(pieces, twist_cos, twist_sin):
        share_count = pieces.shape[1]
        lane_count = pieces.shape[2]
        flatten = pieces.reshape(span_count, share_count * lane_count)
        mixture = jnp.dot(long_forward, flatten, preferred_element_type=jnp.float32)
        mixture = mixture.reshape(2, span_count, share_count, lane_count)
        real_part = mixture[0] * twist_cos + mixture[1] * twist_sin
        imag_part = mixture[1] * twist_cos - mixture[0] * twist_sin
        return jnp.stack([real_part, imag_part]).astype(jnp.bfloat16)

    def long_back(combined_re, combined_im, twist_cos, twist_sin):
        merged_re = combined_re * twist_cos - combined_im * twist_sin
        merged_im = combined_im * twist_cos + combined_re * twist_sin
        share_count = combined_re.shape[1]
        lane_count = combined_re.shape[2]
        stacked = (
            jnp.stack([merged_re, merged_im])
            .astype(jnp.bfloat16)
            .reshape(2 * span_count, share_count * lane_count)
        )
        summed = jnp.dot(long_inverse, stacked, preferred_element_type=jnp.float32) * (
            1.0 / seq_len
        )
        return summed.astype(jnp.bfloat16).reshape(span_count, share_count, lane_count)

    block_product = positions[:, None] * (2 * positions[None, :] + parity) % (2 * blocksize)
    block_angles = block_product.astype(jnp.float32) * (math.pi / blocksize)
    block_cos = jnp.cos(block_angles)
    block_sin = jnp.sin(block_angles)
    forward_mat = jnp.concatenate(
        [
            jnp.concatenate([block_cos, -block_sin], axis=1),
            jnp.concatenate([block_sin, block_cos], axis=1),
        ],
        axis=0,
    ).astype(jnp.bfloat16)
    cos_turned = jnp.transpose(block_cos)
    sin_turned = jnp.transpose(block_sin)
    inverse_mat = jnp.concatenate(
        [
            jnp.concatenate([cos_turned, sin_turned], axis=1),
            jnp.concatenate([-sin_turned, cos_turned], axis=1),
        ],
        axis=0,
    ).astype(jnp.bfloat16)
    twist_product = (parity * blocksize + positions)[None, None, :] * counter[:, None, None]
    twist_angles = twist_product.astype(jnp.float32) * (2.0 * math.pi / seq_len)
    twist_cos = jnp.cos(twist_angles)
    twist_sin = jnp.sin(twist_angles)

    def section_pairs(pieces):
        return first_section(pieces, twist_cos, twist_sin)

    def spectrum(signal):
        arranged = jnp.transpose(signal).reshape(span_count, shares, blocksize)
        twisted = section_pairs(
            lax.all_to_all(arranged, "wide", split_axis=0, concat_axis=0, tiled=True)
        )
        partner = partner_2(twisted, "narrow", 0)
        paired = (signed * twisted.astype(jnp.float32) + partner.astype(jnp.float32)).astype(
            jnp.bfloat16
        )
        joined = jnp.concatenate(
            [paired[0].reshape(row_count, blocksize), paired[1].reshape(row_count, blocksize)],
            axis=1,
        )
        return jnp.dot(joined, forward_mat, preferred_element_type=jnp.float32)

    def invert(spectrum_in):
        unfolded = jnp.dot(spectrum_in, inverse_mat, preferred_element_type=jnp.float32).astype(
            jnp.bfloat16
        )
        partner = partner_2(unfolded, "narrow", 0)
        combined = signed * unfolded.astype(jnp.float32) + partner.astype(jnp.float32)
        comb_re = combined[:, :blocksize].reshape(span_count, shares, blocksize)
        comb_im = combined[:, blocksize:].reshape(span_count, shares, blocksize)
        arranged = long_back(comb_re, comb_im, twist_cos, twist_sin)
        returned = lax.all_to_all(arranged, "wide", split_axis=0, concat_axis=1, tiled=True)
        return jnp.transpose(returned.reshape(channels, blocksize))

    def product(left_side, right_side, conjugate, factor):
        left_re = left_side[..., :blocksize]
        left_im = left_side[..., blocksize:]
        right_re = right_side[..., :blocksize]
        right_im = right_side[..., blocksize:]
        if conjugate:
            real_part = left_re * right_re + left_im * right_im
            imag_part = left_re * right_im - left_im * right_re
        else:
            real_part = left_re * right_re - left_im * right_im
            imag_part = left_re * right_im + left_im * right_re
        return (jnp.concatenate([real_part, imag_part], axis=-1) * factor).astype(jnp.bfloat16)

    kernel_scale = 1.0 / math.sqrt(seq_len)
    input_spectrum = spectrum(inputs)
    kernel_spectrum = spectrum(filter_taps) * kernel_scale
    outputs = invert(product(kernel_spectrum, input_spectrum, False, 1.0))
    grad_spectrum = spectrum(grad_out)
    grad_inputs = invert(product(kernel_spectrum, grad_spectrum, True, 1.0))
    grad_taps = invert(product(input_spectrum, grad_spectrum, True, kernel_scale))
    return (outputs, grad_inputs, grad_taps)


RADIX = 8


def exact_tables(blocksize, seq_len, lanes):
    j = np.arange(blocksize)
    mats = []
    for r in range(2):
        ang = (j[:, None] * (2 * j[None, :] + r) % (2 * blocksize)).astype(np.float32)
        ang = ang * np.float32(math.pi / blocksize)
        cos, sin = np.cos(ang), np.sin(ang)
        mats.append(np.block([[cos, -sin], [sin, cos]]))
    inverse = np.stack(mats).astype(ml_dtypes.bfloat16)
    forward = np.ascontiguousarray(np.transpose(inverse, (0, 2, 1)))
    k1 = np.arange(1, RADIX // 2 + 1)[:, None, None]
    n = np.arange(2)[None, :, None]
    ang = ((n * blocksize + j[None, None, :]) * k1).astype(np.float32)
    ang = ang * np.float32(2.0 * math.pi / seq_len)
    shape = (RADIX // 2, 2, blocksize, lanes)
    cos = np.ascontiguousarray(np.broadcast_to(np.cos(ang)[..., None], shape))
    sin = np.ascontiguousarray(np.broadcast_to(np.sin(ang)[..., None], shape))
    return forward, inverse, cos, sin


def fused_kernel(
    x_ref, f_ref, g_ref, fwd_hbm, inv_hbm, cos_hbm, sin_hbm, o0_ref, o1_ref, o2_ref,
    buf, spec, mix, unf, obuf, fwd, inv, tcos, tsin,
    send_sem, recv_sem, own_sem, osend_sem, orecv_sem, oown_sem, table_sem,
    relay_send_sem, relay_recv_sem,
):
    block, lanes = buf.shape[2], buf.shape[3]
    wide, narrow = lax.axis_index("wide"), lax.axis_index("narrow")
    half, place = wide // 4, wide % 4
    group = lax.axis_index("groups")
    mine = wide * 2 + narrow
    signals = (x_ref, f_ref, g_ref)
    outs = (o0_ref, o1_ref, o2_ref)
    root = float(np.float32(ml_dtypes.bfloat16(math.cos(math.pi / 4))))

    def peer(dh, dp, dc):
        w = (half + dh) % 2 * 4 + (place + dp) % 4
        return w, (narrow + dc) % 2

    offsets = [(dh, dp, dc) for dh in (1, 0) for dp in (0, 1, 2, 3) for dc in (0, 1)]
    others = [o for o in offsets if o != (0, 0, 0)]

    def where(w, c):
        return {"wide": w, "narrow": c}

    def columns(w, c):
        return pl.ds(pl.multiple_of((w % 4 * 2 + c) * lanes, lanes), lanes)

    tables = [
        pltpu.make_async_copy(a, b, table_sem.at[i])
        for i, (a, b) in enumerate(
            ((cos_hbm, tcos), (sin_hbm, tsin), (fwd_hbm, fwd), (inv_hbm, inv))
        )
    ]

    barrier = pltpu.get_barrier_semaphore()
    for o in others:
        w, c = peer(*o)
        pl.semaphore_signal(
            barrier, inc=1, device_id=where(w, c), device_id_type=pl.DeviceIdType.MESH
        )
    pl.semaphore_signal(
        barrier, inc=1, device_id={"groups": 1 - group}, device_id_type=pl.DeviceIdType.MESH
    )
    pl.semaphore_wait(barrier, len(others) + 1)

    far = [i for i, o in enumerate(others) if o[0] == 1]

    def share(g):
        return pl.ds(pl.multiple_of(g * (block // 2), block // 2), block // 2)

    def piece(ref, s, i, g):
        return ref.at[share(g)] if s == 1 and i in far else ref

    def send(s, i):
        w, c = peer(*others[i])
        return pltpu.make_async_remote_copy(
            src_ref=piece(signals[s].at[:, columns(w, c)], s, i, group),
            dst_ref=piece(buf.at[s, mine], s, i, group),
            send_sem=send_sem.at[s, i],
            recv_sem=recv_sem.at[s, mine],
            device_id=where(w, c),
            device_id_type=pl.DeviceIdType.MESH,
        )

    def arrived(s, i):
        w, c = peer(*others[i])
        b = w * 2 + c
        return pltpu.make_async_remote_copy(
            src_ref=piece(buf.at[s, b], s, i, group),
            dst_ref=piece(buf.at[s, b], s, i, group),
            send_sem=send_sem.at[s, i],
            recv_sem=recv_sem.at[s, b],
            device_id=where(w, c),
            device_id_type=pl.DeviceIdType.MESH,
        )

    def relay(i, g):
        w, c = peer(*others[i])
        rows = piece(buf.at[1, w * 2 + c], 1, i, g)
        return pltpu.make_async_remote_copy(
            src_ref=rows,
            dst_ref=rows,
            send_sem=relay_send_sem.at[i],
            recv_sem=relay_recv_sem.at[i],
            device_id={"groups": 1 - group},
            device_id_type=pl.DeviceIdType.MESH,
        )

    def own(s):
        return pltpu.make_async_copy(
            signals[s].at[:, columns(wide, narrow)], buf.at[s, mine], own_sem.at[s]
        )

    def launch(s):
        for i in reversed(range(len(others))):
            send(s, i).start()
        own(s).start()

    def collect(s):
        for i in reversed(range(len(others))):
            arrived(s, i).wait_recv()
            if s == 1 and i in far:
                relay(i, group).start()
        if s == 1:
            for i in far:
                relay(i, 1 - group).wait_recv()
        own(s).wait()

    step = 16

    def forward(s):
        def tile(t, carry):
            rows = pl.ds(pl.multiple_of(t * step, step), step)
            low = pl.ds(pl.multiple_of(t * step + block, step), step)
            halves = []
            for n in range(2):
                a = [buf[s, 2 * i + n, rows, :].astype(jnp.float32) for i in range(RADIX)]
                e = [a[i] + a[i + 4] for i in range(4)]
                d = [a[i] - a[i + 4] for i in range(4)]
                even, odd = e[0] + e[2], e[1] + e[3]
                minus = root * (d[1] - d[3])
                plus = root * (d[1] + d[3])
                raw = [
                    (d[0] + minus, -(d[2] + plus)),
                    (e[0] - e[2], e[3] - e[1]),
                    (d[0] - minus, d[2] - plus),
                    (even - odd, None),
                ]
                got = [(even + odd, None)]
                for k, (re, im) in enumerate(raw):
                    cos, sin = tcos[k, n, rows, :], tsin[k, n, rows, :]
                    if im is None:
                        got.append((re * cos, -(re * sin)))
                    else:
                        got.append((re * cos + im * sin, im * cos - re * sin))
                halves.append(got)
            for k in range(RADIX // 2 + 1):
                cols = slice(k * lanes, (k + 1) * lanes)
                (r0, i0), (r1, i1) = halves[0][k], halves[1][k]
                mix[0, rows, cols] = (r0 + r1).astype(jnp.bfloat16)
                mix[1, rows, cols] = (r0 - r1).astype(jnp.bfloat16)
                if i0 is not None:
                    mix[0, low, cols] = (i0 + i1).astype(jnp.bfloat16)
                    mix[1, low, cols] = (i0 - i1).astype(jnp.bfloat16)
                else:
                    mix[0, low, cols] = jnp.zeros_like(r0, jnp.bfloat16)
                    mix[1, low, cols] = jnp.zeros_like(r0, jnp.bfloat16)
            return carry

        lax.fori_loop(0, block // step, tile, 0)
        multiply(fwd, spec.at[s])

    def multiply(table, result):
        def one(r, carry):
            width = mix.shape[2]
            for first in range(0, width, 256):
                cols = slice(first, min(first + 256, width))
                result[r, :, cols] = jnp.dot(
                    table[r], mix[r, :, cols], preferred_element_type=jnp.float32
                )
            return carry

        lax.fori_loop(0, 2, one, 0)

    def combine(left, right, conjugate):
        def tile(t, carry):
            rows = pl.ds(pl.multiple_of(t * step, step), step)
            low = pl.ds(pl.multiple_of(t * step + block, step), step)
            for r in range(2):
                for k in range(RADIX // 2 + 1):
                    cols = slice(k * lanes, (k + 1) * lanes)
                    lr, li = spec[left, r, rows, cols], spec[left, r, low, cols]
                    rr, ri = spec[right, r, rows, cols], spec[right, r, low, cols]
                    if conjugate:
                        re, im = lr * rr + li * ri, lr * ri - li * rr
                    else:
                        re, im = lr * rr - li * ri, lr * ri + li * rr
                    mix[r, rows, cols] = re.astype(jnp.bfloat16)
                    mix[r, low, cols] = im.astype(jnp.bfloat16)
            return carry

        lax.fori_loop(0, block // step, tile, 0)

    scale = 2.0 ** -18
    side = (1 - 2 * half).astype(jnp.float32) * (2.0 * scale)

    def inverse(o, left, right, conjugate):
        combine(left, right, conjugate)
        multiply(inv, unf)

        def tile(t, carry):
            rows = pl.ds(pl.multiple_of(t * step, step), step)
            low = pl.ds(pl.multiple_of(t * step + block, step), step)
            for n in range(2):
                sign = 1 if n == 0 else -1
                zero = slice(0, lanes)
                parts = [(unf[0, rows, zero] + sign * unf[1, rows, zero]) * scale]
                for k in range(RADIX // 2):
                    cols = slice((k + 1) * lanes, (k + 2) * lanes)
                    re = unf[0, rows, cols] + sign * unf[1, rows, cols]
                    im = unf[0, low, cols] + sign * unf[1, low, cols]
                    cos, sin = tcos[k, n, rows, :], tsin[k, n, rows, :]
                    mre = re * cos - im * sin
                    if k == RADIX // 2 - 1:
                        parts.append(mre * scale)
                    else:
                        factor = 2.0 * scale if k == 1 else side
                        parts.append((mre * factor, (im * cos + re * sin) * factor))
                a, (r1, i1), (r2, i2), (r3, i3), b = parts
                top, bottom = a + b, a - b
                left_, right_ = root * (r1 - r3), root * (i1 + i3)
                values = (
                    top + r2 + (r1 + r3),
                    bottom - i2 + (left_ - right_),
                    top - r2 + (i3 - i1),
                    bottom + i2 - (left_ + right_),
                )
                for u in range(4):
                    obuf[o, 2 * u + n, rows, :] = values[u].astype(jnp.bfloat16)
            return carry

        lax.fori_loop(0, block // step, tile, 0)

    near = [(dp, dc) for dp in range(4) for dc in range(2)][1:]

    def give(o, i):
        w, c = peer(0, *near[i])
        return pltpu.make_async_remote_copy(
            src_ref=obuf.at[o, w % 4 * 2 + c],
            dst_ref=outs[o].at[:, columns(wide, narrow)],
            send_sem=osend_sem.at[o, i],
            recv_sem=orecv_sem.at[o, place * 2 + narrow],
            device_id=where(w, c),
            device_id_type=pl.DeviceIdType.MESH,
        )

    def taken(o, i):
        w, c = peer(0, *near[i])
        return pltpu.make_async_remote_copy(
            src_ref=obuf.at[o, w % 4 * 2 + c],
            dst_ref=outs[o].at[:, columns(w, c)],
            send_sem=osend_sem.at[o, i],
            recv_sem=orecv_sem.at[o, w % 4 * 2 + c],
            device_id=where(w, c),
            device_id_type=pl.DeviceIdType.MESH,
        )

    def keep(o):
        return pltpu.make_async_copy(
            obuf.at[o, place * 2 + narrow],
            outs[o].at[:, columns(wide, narrow)],
            oown_sem.at[o],
        )

    def deliver(o):
        for i in reversed(range(len(near))):
            give(o, i).start()
        keep(o).start()

    launch(1)
    launch(0)
    launch(2)
    for t in tables:
        t.start()
    for t in tables:
        t.wait()
    collect(1)
    forward(1)
    collect(0)
    forward(0)
    inverse(0, 1, 0, False)
    deliver(0)
    collect(2)
    forward(2)
    inverse(1, 1, 2, True)
    deliver(1)
    inverse(2, 0, 2, True)
    deliver(2)
    for i in far:
        relay(i, group).wait_send()
    for s in range(3):
        for i in range(len(others)):
            send(s, i).wait_send()
    for o in range(3):
        for i in range(len(near)):
            give(o, i).wait_send()
            taken(o, i).wait_recv()
        keep(o).wait()


def settle_kernel(a0, a1, a2, o0, o1, o2, held, load_sem, store_sem):
    pairs = ((a0, o0), (a1, o1), (a2, o2))
    loads = [
        pltpu.make_async_copy(a, held.at[i], load_sem.at[i]) for i, (a, _) in enumerate(pairs)
    ]
    stores = [
        pltpu.make_async_copy(held.at[i], o, store_sem.at[i]) for i, (_, o) in enumerate(pairs)
    ]
    for load in loads:
        load.start()
    for load, store in zip(loads, stores):
        load.wait()
        store.start()
    for store in stores:
        store.wait()


def on_device_fused(inputs, filter_taps, grad_out):
    block, channels = inputs.shape
    lanes = channels // RADIX
    tables = exact_tables(block, RADIX * 2 * block, lanes)
    width = (RADIX // 2 + 1) * lanes
    out = jax.ShapeDtypeStruct(inputs.shape, jnp.bfloat16)
    anywhere = pl.BlockSpec(memory_space=pltpu.HBM)
    results = pl.pallas_call(
        fused_kernel,
        out_shape=(out, out, out),
        in_specs=[anywhere] * 7,
        out_specs=(anywhere,) * 3,
        scratch_shapes=[
            pltpu.VMEM((3, 2 * RADIX, block, lanes), jnp.bfloat16),
            pltpu.VMEM((3, 2, 2 * block, width), jnp.float32),
            pltpu.VMEM((2, 2 * block, width), jnp.bfloat16),
            pltpu.VMEM((2, 2 * block, width), jnp.float32),
            pltpu.VMEM((3, RADIX, block, lanes), jnp.bfloat16),
            pltpu.VMEM((2, 2 * block, 2 * block), jnp.bfloat16),
            pltpu.VMEM((2, 2 * block, 2 * block), jnp.bfloat16),
            pltpu.VMEM((RADIX // 2, 2, block, lanes), jnp.float32),
            pltpu.VMEM((RADIX // 2, 2, block, lanes), jnp.float32),
            pltpu.SemaphoreType.DMA((3, 15)),
            pltpu.SemaphoreType.DMA((3, 16)),
            pltpu.SemaphoreType.DMA((3,)),
            pltpu.SemaphoreType.DMA((3, 7)),
            pltpu.SemaphoreType.DMA((3, 8)),
            pltpu.SemaphoreType.DMA((3,)),
            pltpu.SemaphoreType.DMA((4,)),
            pltpu.SemaphoreType.DMA((8,)),
            pltpu.SemaphoreType.DMA((8,)),
        ],
        compiler_params=pltpu.CompilerParams(
            collective_id=0, has_side_effects=True, vmem_limit_bytes=60 * 2**20
        ),
    )(inputs, filter_taps, grad_out, *tables)
    return pl.pallas_call(
        settle_kernel,
        out_shape=(out, out, out),
        in_specs=[anywhere] * 3,
        out_specs=(anywhere,) * 3,
        scratch_shapes=[
            pltpu.VMEM((3,) + inputs.shape, jnp.bfloat16),
            pltpu.SemaphoreType.DMA((3,)),
            pltpu.SemaphoreType.DMA((3,)),
        ],
    )(*results)


def solution(mesh):
    in_specs = (
        P(("groups", "wide", "narrow"), None),
        P(("wide", "narrow"), None),
        P(("groups", "wide", "narrow"), None),
    )
    out_specs = (P(("groups", "wide", "narrow"), None),) * 3
    body = on_device_fused if (mesh.shape["wide"], mesh.shape["groups"]) == (RADIX, 2) else on_device
    return jax.shard_map(
        body, mesh=mesh, in_specs=in_specs, out_specs=out_specs, check_vma=False
    )
```
